256 devices in a mesh: expert: 32 (over x_hi, z, core), shard: 8 (over x_lo, y).
Axes of the slice: x: 4 (x_hi: 2, x_lo: 2; x = x_hi * 2 + x_lo), y: 4, z: 8, core: 2. Of those that a mesh axis runs over, the one named last changes fastest.
Arguments:
- train_acts: bfloat16 [65536, 2048], P(('expert', 'shard')), may hold values from -6 to 6
- train_grads: bfloat16 [65536, 768], P(('expert', 'shard')), may hold values from -6 to 6
- slot_counts: int32 [256, 2, 32], P(('expert', 'shard')), may hold values from 1 to 4, as said below
- query_acts: bfloat16 [2, 32, 64, 2048], P(None, 'expert'), may hold values from -6 to 6
- query_grads: bfloat16 [2, 32, 64, 768], P(None, 'expert'), may hold values from -6 to 6
- query_ids: int32 [2, 32, 64], P(None, 'expert'), may hold values from 0 to 7
- basis_in: bfloat16 [2, 32, 2048, 2048], P(None, 'expert', None, 'shard'), may hold values from -0.125 to 0.125
- eigen_vals: bfloat16 [2, 32, 768, 2048], P(None, 'expert', None, 'shard'), may hold values from 0.5 to 8
- basis_out: bfloat16 [2, 32, 768, 768], P(None, 'expert'), may hold values from -0.21875 to 0.21875
Outputs:
- influence: float32 [8, 65536], P(None, ('expert', 'shard'))
The draws below stay inside these ranges and needn't reach their ends.
Inputs may be any that keep to these rules, and one draw needn't show every extreme that they name: `slot_counts`: in every turn one expert has all 4 slots live from every device group.
All inputs are finite; a program needn't handle non-finite values.
Results may differ from the reference program's by a relative error of at most 0.0055.
Values may be sent and summed in bfloat16 or wider, within the bound.
No kernel may reach another device: no remote copies, remote signals or barrier semaphores. Data moves between devices by JAX's collectives and lax.ppermute only.
A program may use at most 192 MiB of HBM per device.

```python
import math
import jax
import jax.numpy as jnp
from jax import lax

HIDDEN_SIZE = 2048
INNER = 768
QUERIES = 8
QROWS = 64
SLOTS = 4
TURNS = 2
EXPERTS = 32
GROUPS = 256
ROWS = 65536


def draw_slot_counts(key, part):
    first_key, second_key = jax.random.split(jax.random.fold_in(key, 11))
    base_counts = jax.random.randint(first_key, (GROUPS, TURNS, EXPERTS), 1, SLOTS + 1)
    full_expert = jax.random.randint(second_key, (TURNS,), 0, EXPERTS)
    expert_ids = jnp.arange(EXPERTS)[None, None, :]
    return jnp.where(expert_ids == full_expert[None, :, None], SLOTS, base_counts).astype(jnp.int32)


def with_ends(entries, own_key, smallest, largest):
    longest = entries.shape.index(max(entries.shape))
    spots = []
    for shift in (0, 1):
        where = [jax.random.randint(jax.random.fold_in(own_key, axis), (), 0, length) for axis, length in enumerate(entries.shape)]
        where[longest] = (where[longest] + shift) % entries.shape[longest]
        spots.append(tuple(where))
    return entries.at[spots[0]].set(smallest).at[spots[1]].set(largest)


def block_scale(key, shape, cuts, least, largest):
    def one(axis_at, shards_of):
        heights = jax.random.uniform(jax.random.fold_in(jax.random.fold_in(key, 6), axis_at), (shards_of,), jnp.float32, least / len(cuts), largest / len(cuts))
        return jnp.repeat(jnp.exp(heights), shape[axis_at] // shards_of).reshape((-1,) + (1,) * (len(shape) - axis_at - 1))

    factor_of = one(*cuts[0])
    for cut in cuts[1:]:
        factor_of = factor_of * one(*cut)
    return factor_of


def gaussian(own_key, dims, scale, most, shards=(), dtype=jnp.bfloat16):
    values = jax.random.normal(own_key, dims, jnp.float32) * scale
    if len(shards) > 0:
        values = block_scale(own_key, dims, shards, -0.22, 0.18) * values
    return jnp.clip(values, min=-most, max=most).astype(dtype)


def setup_inputs(seed: int = 0) -> dict:
    keys = jax.random.split(jax.random.key(seed), 10)
    return {
        "train_acts": gaussian(keys[0], (ROWS, HIDDEN_SIZE), 1.0, 6.0, ((0, 256),)),
        "train_grads": gaussian(keys[1], (ROWS, INNER), 1.0, 6.0, ((0, 256),)),
        "slot_counts": draw_slot_counts(jax.random.fold_in(keys[9], 71), 0),
        "query_acts": gaussian(keys[3], (TURNS, EXPERTS, QROWS, HIDDEN_SIZE), 1.0, 6.0, ((1, 32),)),
        "query_grads": gaussian(keys[4], (TURNS, EXPERTS, QROWS, INNER), 1.0, 6.0, ((1, 32),)),
        "query_ids": with_ends(jax.random.randint(keys[5], (TURNS, EXPERTS, QROWS), 0, QUERIES), jax.random.fold_in(keys[5], 1), 0, QUERIES - 1).astype(jnp.int32),
        "basis_in": gaussian(keys[6], (TURNS, EXPERTS, HIDDEN_SIZE, HIDDEN_SIZE), HIDDEN_SIZE ** -0.5, 0.125, ((1, 32), (3, 8))),
        "eigen_vals": jnp.clip(jnp.exp(math.log(8.0) - 2.7725887 * jax.random.uniform(keys[7], (TURNS, EXPERTS, INNER, HIDDEN_SIZE), jnp.float32) ** block_scale(keys[7], (TURNS, EXPERTS, INNER, HIDDEN_SIZE), ((1, 32), (3, 8)), -0.2, 0.2)), 0.5, 8.0).astype(jnp.bfloat16),
        "basis_out": gaussian(keys[8], (TURNS, EXPERTS, INNER, INNER), INNER ** -0.5, 0.21875, ((1, 32),)),
    }


DAMPING = 0.05

def reference(train_acts, train_grads, slot_counts, query_acts, query_grads, query_ids, basis_in, eigen_vals, basis_out):
    groups = slot_counts.shape[0]
    norm_scale = 1.0 / math.sqrt(INNER * HIDDEN_SIZE)
    acts_grouped = train_acts.reshape(groups, TURNS, EXPERTS, SLOTS, HIDDEN_SIZE)
    grads_grouped = train_grads.reshape(groups, TURNS, EXPERTS, SLOTS, INNER)
    queries = jnp.arange(QUERIES)
    turn_scores = []
    for turn_index in range(TURNS):

        def one_expert(expert_items):
            in_basis, out_basis, eigen_part, q_acts, q_grads, q_ids, act_rows, grad_rows = expert_items
            weight = norm_scale / (eigen_part.astype(jnp.float32) + DAMPING)
            chosen = (q_ids[:, None] == queries[None, :]).astype(jnp.bfloat16)
            query_u = jnp.dot(q_grads, out_basis, preferred_element_type=jnp.float32).astype(jnp.bfloat16)
            query_v = jnp.dot(q_acts, in_basis, preferred_element_type=jnp.float32).astype(jnp.bfloat16)
            stacked = (query_u[:, :, None] * chosen[:, None, :]).reshape(query_u.shape[0], INNER * QUERIES)
            rotated = lax.dot_general(stacked, query_v, (((0,), (0,)), ((), ())), preferred_element_type=jnp.float32)
            precond = (rotated.reshape(INNER, QUERIES, HIDDEN_SIZE) * weight[:, None, :]).astype(jnp.bfloat16)
            flat_precond = precond.reshape(INNER, QUERIES * HIDDEN_SIZE)
            flat_acts = act_rows.reshape(groups * SLOTS, HIDDEN_SIZE)
            flat_grads = grad_rows.reshape(groups * SLOTS, INNER)
            train_u = jnp.dot(flat_grads, out_basis, preferred_element_type=jnp.float32).astype(jnp.bfloat16)
            train_v = jnp.dot(flat_acts, in_basis, preferred_element_type=jnp.float32).astype(jnp.bfloat16)
            project = jnp.dot(train_u, flat_precond, preferred_element_type=jnp.float32).reshape(groups * SLOTS, QUERIES, HIDDEN_SIZE)
            scores = jnp.einsum('rqj,rj->qr', project, train_v.astype(jnp.float32))
            return scores.reshape(QUERIES, groups, SLOTS)
        items = (basis_in[turn_index], basis_out[turn_index], eigen_vals[turn_index], query_acts[turn_index], query_grads[turn_index], query_ids[turn_index], jnp.swapaxes(acts_grouped[:, turn_index], 0, 1), jnp.swapaxes(grads_grouped[:, turn_index], 0, 1))
        scores = lax.map(one_expert, items)
        live_mask = jnp.arange(SLOTS)[None, None, :] < jnp.swapaxes(slot_counts[:, turn_index, :], 0, 1)[:, :, None]
        scores = jnp.where(live_mask[:, None, :, :], scores, 0.0)
        turn_scores.append(scores.transpose(1, 2, 0, 3))
    summed = jnp.stack(turn_scores, axis=2)
    return summed.reshape(QUERIES, groups * TURNS * EXPERTS * SLOTS)
```

```python
import functools
import math

import jax
import jax.numpy as jnp
from jax import lax
from jax.experimental import pallas as pl
from jax.experimental.pallas import tpu as pltpu
from jax.sharding import Mesh, PartitionSpec as P

HIDDEN_SIZE = 2048
INNER = 768
QUERIES = 8
SLOTS = 4
TURNS = 2
DAMPING = 0.05

SIZES = (2, 8, 2, 2, 4)
AXES = ("xh", "z", "core", "xl", "y")


def flat_index(xh, z, core, xl, y):
    return (((xh * 8 + z) * 2 + core) * 2 + xl) * 4 + y


def route_groups():
    groups = []
    for core in range(2):
        for low in range(2):
            turn_y = (low, 3 - low)
            groups.append(
                [
                    flat_index(xh, z, core, xl, turn_y[k])
                    for k in range(2)
                    for xh in range(2)
                    for z in range(8)
                    for xl in range(2)
                ]
            )
    return groups


def moves(home_step, guest_step):
    pairs = []
    for core in range(2):
        for xl in range(2):
            for y in range(4):
                step = home_step if core == xl else guest_step
                if step is not None:
                    pairs.append(((core * 2 + xl) * 4 + y, step(core, xl, y)))
    return pairs


def place(core, xl, y):
    return (core * 2 + xl) * 4 + y


def cross_step(core, xl, y):
    return place(1 - core, 1 - xl, y)


def outer_step(core, xl, y):
    return place(core, xl, 3 - y)


def inner_step(core, xl, y):
    return place(core, xl, y ^ 1)


def send(x, home_step, guest_step):
    return lax.ppermute(x, ("core", "xl", "y"), moves(home_step, guest_step))


def other_core(x):
    return lax.ppermute(x, "core", [(0, 1), (1, 0)])


def rotate_kernel(rows_a, rows_b, b_out, u_ref):
    for n, rows in enumerate((rows_a, rows_b)):
        u_ref[pl.ds(n * 256, 256), :] = jnp.dot(
            rows[:, HIDDEN_SIZE:], b_out[...], preferred_element_type=jnp.float32
        ).astype(jnp.bfloat16)


def rotate(rows_a, rows_b, b_out):
    return pl.pallas_call(
        rotate_kernel,
        out_shape=jax.ShapeDtypeStruct((512, INNER), jnp.bfloat16),
        in_specs=[pl.BlockSpec(memory_space=pltpu.VMEM)] * 3,
        out_specs=pl.BlockSpec(memory_space=pltpu.VMEM),
        compiler_params=pltpu.CompilerParams(vmem_limit_bytes=24 << 20),
        cost_estimate=pl.CostEstimate(
            flops=2 * 512 * INNER * INNER, bytes_accessed=5 << 20, transcendentals=0
        ),
    )(rows_a, rows_b, b_out)


def score_kernel(choice, home_ref, rows_a, rows_b, u_ref, qu_ref, q_acts, ids, before, *refs):
    n_pairs = len(choice)
    block_refs = refs[: sum(choice)]
    out_ref, held, sems = refs[sum(choice) :]
    home = home_ref[0] == 1

    def fetch(n, ref):
        return pltpu.make_async_copy(ref, held.at[n], sems.at[n])

    at = 0
    plan = []
    for n in range(n_pairs):
        plan.append(block_refs[at : at + choice[n]])
        at += choice[n]
        if choice[n] == 1:
            fetch(n, plan[n][0]).start()
        else:

            @pl.when(home)
            def _(n=n):
                fetch(n, plan[n][0]).start()

            @pl.when(jnp.logical_not(home))
            def _(n=n):
                fetch(n, plan[n][1]).start()

    norm_scale = 1.0 / math.sqrt(INNER * HIDDEN_SIZE)
    lanes = lax.broadcasted_iota(jnp.int32, (512, QUERIES), 1)
    total = before[...]
    for n in range(n_pairs):
        fetch(n, plan[n][0]).wait()
        basis = held[n, :HIDDEN_SIZE, :]
        weight = norm_scale / (held[n, HIDDEN_SIZE:, :].astype(jnp.float32) + DAMPING)
        query_v = jnp.dot(q_acts[...], basis, preferred_element_type=jnp.float32)
        train_v = jnp.concatenate(
            [
                jnp.dot(rows[:, :HIDDEN_SIZE], basis, preferred_element_type=jnp.float32)
                for rows in (rows_a, rows_b)
            ],
            axis=0,
        )
        train_v = train_v.astype(jnp.bfloat16).astype(jnp.float32)
        for q in range(QUERIES):
            chosen_v = jnp.where(ids[...] == q, query_v, 0.0).astype(jnp.bfloat16)
            rotated = jnp.dot(qu_ref[...], chosen_v, preferred_element_type=jnp.float32)
            precond = (rotated * weight).astype(jnp.bfloat16)
            project = jnp.dot(u_ref[...], precond, preferred_element_type=jnp.float32)
            score = jnp.sum(project * train_v, axis=1, keepdims=True)
            total = total + jnp.where(lanes == q, score, 0.0)
    out_ref[...] = total


def score(home, rows_a, rows_b, u, qu_t, q_acts, ids, before, blocks):
    choice = tuple(len(b) for b in blocks)
    flat = [x for b in blocks for x in b]
    width = flat[0].shape[1]
    n = len(blocks)
    vmem = pl.BlockSpec(memory_space=pltpu.VMEM)
    return pl.pallas_call(
        functools.partial(score_kernel, choice),
        out_shape=jax.ShapeDtypeStruct((512, QUERIES), jnp.float32),
        in_specs=[pl.BlockSpec(memory_space=pltpu.SMEM)]
        + [vmem] * 7
        + [pl.BlockSpec(memory_space=pl.ANY)] * len(flat),
        out_specs=vmem,
        scratch_shapes=[
            pltpu.VMEM((n, HIDDEN_SIZE + INNER, width), jnp.bfloat16),
            pltpu.SemaphoreType.DMA((n,)),
        ],
        compiler_params=pltpu.CompilerParams(vmem_limit_bytes=40 << 20),
        cost_estimate=pl.CostEstimate(
            flops=n * 2 * 512 * width * (HIDDEN_SIZE + QUERIES * INNER),
            bytes_accessed=(4 + 2 * n) << 20,
            transcendentals=0,
        ),
    )(home, rows_a, rows_b, u, qu_t, q_acts, ids, before, *flat)


def on_device(
    train_acts,
    train_grads,
    slot_counts,
    query_acts,
    query_grads,
    query_ids,
    basis_in,
    eigen_vals,
    basis_out,
):
    core, xl, y = lax.axis_index("core"), lax.axis_index("xl"), lax.axis_index("y")
    turn = y // 2
    is_home = core == xl
    home = is_home.astype(jnp.int32).reshape(1)
    groups = route_groups()

    def pick(array, which):
        return lax.dynamic_index_in_dim(array, which, 0, keepdims=False)[0]

    def weights(which):
        return jnp.concatenate([pick(basis_in, which), pick(eigen_vals, which)], axis=0)

    far, own = weights(1 - turn), weights(turn)
    first = send(far, outer_step, cross_step)
    second = send(own, inner_step, cross_step)

    train_acts, train_grads, _, _ = lax.optimization_barrier((train_acts, train_grads, far, own))
    rows = jnp.concatenate(
        [
            train_acts.reshape(64, SLOTS, HIDDEN_SIZE),
            train_grads.reshape(64, SLOTS, INNER),
        ],
        axis=2,
    )
    mine = lax.all_to_all(rows, AXES, 0, 0, axis_index_groups=groups, tiled=True)

    third = send(first, inner_step, outer_step)
    fourth = send(second, None, inner_step)
    fifth = send(third, None, inner_step)

    mine, third, fourth = lax.optimization_barrier((mine, third, fourth))
    mine = mine.reshape(256, HIDDEN_SIZE + INNER)
    theirs = other_core(mine)

    query_acts, query_grads, query_ids, basis_out, second = lax.optimization_barrier(
        (query_acts, query_grads, query_ids, basis_out, second)
    )

    def from_home(x):
        return jnp.where(is_home, x, other_core(x))

    q_acts = from_home(pick(query_acts, turn))
    q_grads = from_home(pick(query_grads, turn))
    q_ids = from_home(pick(query_ids, turn)).reshape(-1, 1)
    b_out = from_home(pick(basis_out, turn))
    qu_t = jnp.dot(q_grads, b_out, preferred_element_type=jnp.float32).astype(jnp.bfloat16).T

    u = rotate(mine, theirs, b_out)
    total = jnp.zeros((512, QUERIES), jnp.float32)
    for blocks in (((second,), (third,)), ((own, fourth),), ((first, fifth),)):
        total = score(home, mine, theirs, u, qu_t, q_acts, q_ids, total, blocks)
    mine_sum = total[:256] + other_core(total[256:])
    back = lax.all_to_all(
        mine_sum.reshape(64, SLOTS, QUERIES), AXES, 0, 0, axis_index_groups=groups, tiled=True
    )
    counts = slot_counts[0].reshape(64)
    live = jnp.arange(SLOTS)[None, :] < counts[:, None]
    return jnp.where(live[:, :, None], back, 0.0).reshape(256, QUERIES).T


def solution(mesh):
    grid = Mesh(mesh.devices.reshape(SIZES), AXES)
    expert, shard = ("xh", "z", "core"), ("xl", "y")
    whole = expert + shard
    in_specs = (
        P(whole, None),
        P(whole, None),
        P(whole, None, None),
        P(None, expert, None, None),
        P(None, expert, None, None),
        P(None, expert, None),
        P(None, expert, None, shard),
        P(None, expert, None, shard),
        P(None, expert, None, None),
    )
    return jax.shard_map(
        on_device, mesh=grid, in_specs=in_specs, out_specs=P(None, whole), check_vma=False
    )
```

```python
import functools
import math

import jax
import jax.numpy as jnp
from jax import lax
from jax.experimental import pallas as pl
from jax.experimental.pallas import tpu as pltpu
from jax.sharding import Mesh, PartitionSpec as P

HIDDEN_SIZE = 2048
INNER = 768
QUERIES = 8
SLOTS = 4
TURNS = 2
DAMPING = 0.05

SIZES = (2, 8, 2, 2, 4)
AXES = ("xh", "z", "core", "xl", "y")


def flat_index(xh, z, core, xl, y):
    return (((xh * 8 + z) * 2 + core) * 2 + xl) * 4 + y


def route_groups():
    groups = []
    for core in range(2):
        for low in range(2):
            turn_y = (low, 3 - low)
            groups.append(
                [
                    flat_index(xh, z, core, xl, turn_y[k])
                    for k in range(2)
                    for xh in range(2)
                    for z in range(8)
                    for xl in range(2)
                ]
            )
    return groups


def moves(home_step, guest_step):
    pairs = []
    for core in range(2):
        for xl in range(2):
            for y in range(4):
                step = home_step if core == xl else guest_step
                if step is not None:
                    pairs.append(((core * 2 + xl) * 4 + y, step(core, xl, y)))
    return pairs


def place(core, xl, y):
    return (core * 2 + xl) * 4 + y


def cross_step(core, xl, y):
    return place(1 - core, 1 - xl, y)


def outer_step(core, xl, y):
    return place(core, xl, 3 - y)


def inner_step(core, xl, y):
    return place(core, xl, y ^ 1)


def send(x, home_step, guest_step):
    return lax.ppermute(x, ("core", "xl", "y"), moves(home_step, guest_step))


def other_core(x):
    return lax.ppermute(x, "core", [(0, 1), (1, 0)])


def load(pairs, sems):
    copies = [
        pltpu.make_async_copy(src, dst, sems.at[n]) for n, (src, dst) in enumerate(pairs)
    ]
    for each in copies:
        each.start()
    for each in copies:
        each.wait()


def through(chunks, sems):
    inward = [
        pltpu.make_async_copy(src, mid, sems.at[0, n]) for n, (src, mid, _) in enumerate(chunks)
    ]
    outward = [
        pltpu.make_async_copy(mid, dst, sems.at[1, n]) for n, (_, mid, dst) in enumerate(chunks)
    ]
    for each in inward:
        each.start()
    for before, after in zip(inward, outward):
        before.wait()
        after.start()
    for each in outward:
        each.wait()


def block_kernel(which_ref, basis, eigen, after, block, held, sems):
    which = which_ref[0]
    chunks = []
    for start in range(0, HIDDEN_SIZE, 512):
        span = pl.ds(start, 512)
        chunks.append((basis.at[which, 0, span], held.at[span], block.at[span]))
    span = pl.ds(HIDDEN_SIZE, INNER)
    chunks.append((eigen.at[which, 0], held.at[span], block.at[span]))
    through(chunks, sems)


def query_pack_kernel(
    turn_ref, ids, q_acts, q_grads, b_out, after, q_pack, b_pack, q_held, b_held, sems
):
    turn = turn_ref[0]
    id_row = jnp.where(turn == 0, ids[0], ids[1]).astype(jnp.float32)
    b_held[INNER + 64 :, :] = jnp.zeros((16, INNER), jnp.bfloat16)
    b_held[INNER + 64 :, :64] = jnp.broadcast_to(id_row, (16, 64)).astype(jnp.bfloat16)
    load(
        [
            (q_acts.at[turn, 0], q_held),
            (b_out.at[turn, 0], b_held.at[pl.ds(0, INNER)]),
            (q_grads.at[turn, 0], b_held.at[pl.ds(INNER, 64)]),
        ],
        sems,
    )
    load([(q_held, q_pack), (b_held, b_pack)], sems)


def rows_kernel(acts, grads, after, rows):
    rows[:, :, :HIDDEN_SIZE] = acts[...].reshape(64, SLOTS, HIDDEN_SIZE)
    rows[:, :, HIDDEN_SIZE:] = grads[...].reshape(64, SLOTS, INNER)


VMEM = pl.BlockSpec(memory_space=pltpu.VMEM)
HBM = pl.BlockSpec(memory_space=pltpu.HBM)
ANY = pl.BlockSpec(memory_space=pl.ANY)
SMEM = pl.BlockSpec(memory_space=pltpu.SMEM)
BLOCK = jax.ShapeDtypeStruct((HIDDEN_SIZE + INNER, 256), jnp.bfloat16)


def pack_block(which, basis, eigen, after):
    return pl.pallas_call(
        block_kernel,
        out_shape=BLOCK,
        in_specs=[SMEM, HBM, HBM, ANY],
        out_specs=HBM,
        scratch_shapes=[pltpu.VMEM(BLOCK.shape, BLOCK.dtype), pltpu.SemaphoreType.DMA((2, 5))],
        compiler_params=pltpu.CompilerParams(vmem_limit_bytes=60 << 20),
    )(which, basis, eigen, after)


def pack_query(turn, ids, q_acts, q_grads, b_out, after):
    return pl.pallas_call(
        query_pack_kernel,
        out_shape=[
            jax.ShapeDtypeStruct((64, HIDDEN_SIZE), jnp.bfloat16),
            jax.ShapeDtypeStruct((INNER + 80, INNER), jnp.bfloat16),
        ],
        in_specs=[SMEM, VMEM] + [HBM] * 3 + [ANY],
        out_specs=[ANY] * 2,
        scratch_shapes=[
            pltpu.VMEM((64, HIDDEN_SIZE), jnp.bfloat16),
            pltpu.VMEM((INNER + 80, INNER), jnp.bfloat16),
            pltpu.SemaphoreType.DMA((3,)),
        ],
        compiler_params=pltpu.CompilerParams(vmem_limit_bytes=60 << 20),
    )(turn, ids, q_acts, q_grads, b_out, after)


def pack_rows(acts, grads, after):
    return pl.pallas_call(
        rows_kernel,
        out_shape=jax.ShapeDtypeStruct((64, SLOTS, HIDDEN_SIZE + INNER), jnp.bfloat16),
        in_specs=[VMEM, VMEM, ANY],
        out_specs=VMEM,
        compiler_params=pltpu.CompilerParams(vmem_limit_bytes=60 << 20),
    )(acts, grads, after)


def query_kernel(
    home_ref, q_own, q_other, b_own, b_other, q_acts, b_out, qu_ref, ids_ref, b_pack, sems
):
    home = home_ref[0] == 1
    options = [((b, b_pack), (q, q_acts)) for q, b in ((q_own, b_own), (q_other, b_other))]
    each_option(home, options, lambda pairs: load(pairs, sems))
    b_out[...] = b_pack[:INNER, :]
    rotated = jnp.dot(
        b_pack[INNER : INNER + 64, :], b_out[...], preferred_element_type=jnp.float32
    )
    turned = jnp.concatenate([rotated, jnp.zeros_like(rotated)], axis=0).T
    qu_ref[...] = turned[:, :64].astype(jnp.bfloat16)
    ids = b_pack[INNER + 64 : INNER + 80, :].astype(jnp.float32)[:1, :128]
    ids_ref[...] = jnp.broadcast_to(ids, (128, 128)).T[:64, :]


def query(home, q_own, q_other, b_own, b_other):
    bf16 = jnp.bfloat16
    return pl.pallas_call(
        query_kernel,
        out_shape=[
            jax.ShapeDtypeStruct((64, HIDDEN_SIZE), bf16),
            jax.ShapeDtypeStruct((INNER, INNER), bf16),
            jax.ShapeDtypeStruct((INNER, 64), bf16),
            jax.ShapeDtypeStruct((64, 128), jnp.float32),
        ],
        in_specs=[SMEM] + [ANY] * 4,
        out_specs=[VMEM] * 4,
        scratch_shapes=[
            pltpu.VMEM((INNER + 80, INNER), bf16),
            pltpu.SemaphoreType.DMA((2,)),
        ],
        compiler_params=pltpu.CompilerParams(vmem_limit_bytes=24 << 20),
        cost_estimate=pl.CostEstimate(
            flops=2 * 64 * INNER * INNER, bytes_accessed=5 << 20, transcendentals=0
        ),
    )(home, q_own, q_other, b_own, b_other)


def each_option(home, options, act):
    if len(options) == 1:
        act(options[0])
    else:
        pl.when(home)(lambda: act(options[0]))
        pl.when(jnp.logical_not(home))(lambda: act(options[1]))


def fetch_blocks(home, choice, refs, held, sems):
    plan, at = [], 0
    for n, count in enumerate(choice):
        plan.append(
            [pltpu.make_async_copy(ref, held.at[n], sems.at[n]) for ref in refs[at : at + count]]
        )
        each_option(home, plan[n], lambda copy: copy.start())
        at += count
    return plan


def block_weight(held, n):
    norm_scale = 1.0 / math.sqrt(INNER * HIDDEN_SIZE)
    return norm_scale / (held[n, HIDDEN_SIZE:, :].astype(jnp.float32) + DAMPING)


def rotate_acts(acts, basis):
    train_v = jnp.dot(acts, basis, preferred_element_type=jnp.float32)
    return train_v.astype(jnp.bfloat16).astype(jnp.float32)


def precondition(qu_ref, ids_ref, query_v, weight, q):
    chosen_v = jnp.where(ids_ref[:, :1] == q, query_v, 0.0).astype(jnp.bfloat16)
    rotated = jnp.dot(qu_ref[...], chosen_v, preferred_element_type=jnp.float32)
    return (rotated * weight).astype(jnp.bfloat16)


def add_score(total, q, u, precond, train_v):
    lanes = lax.broadcasted_iota(jnp.int32, total.shape, 1)
    project = jnp.dot(u, precond, preferred_element_type=jnp.float32)
    score = jnp.sum(project * train_v, axis=1, keepdims=True)
    return total + jnp.where(lanes == q, score, 0.0)


def add_blocks(home, plan, held, acts, u_ref, qu_ref, ids_ref, q_acts, total, kept=None):
    for n, options in enumerate(plan):
        each_option(home, options, lambda copy: copy.wait())
        basis = held[n, :HIDDEN_SIZE, :]
        weight = block_weight(held, n)
        query_v = jnp.dot(q_acts[...], basis, preferred_element_type=jnp.float32)
        train_v = rotate_acts(acts[...], basis)
        for q in range(QUERIES):
            precond = precondition(qu_ref, ids_ref, query_v, weight, q)
            if kept is not None:
                kept[n, pl.ds(q * INNER, INNER), :] = precond
            total = add_score(total, q, u_ref[...], precond, train_v)
    return total


def unpack_rows(rows, b_out, acts, u_ref):
    acts[...] = rows[:, :, :HIDDEN_SIZE].reshape(256, HIDDEN_SIZE)
    u_ref[...] = jnp.dot(
        rows[:, :, HIDDEN_SIZE:].reshape(256, INNER),
        b_out[...],
        preferred_element_type=jnp.float32,
    ).astype(jnp.bfloat16)


def early_kernel(choice, home_ref, rows, b_out, qu_ref, ids_ref, q_acts, *refs):
    count = sum(choice)
    mine_ref, acts, u_ref, kept, held, sems = refs[count:]
    home = home_ref[0] == 1
    plan = fetch_blocks(home, choice, refs[:count], held, sems)
    unpack_rows(rows, b_out, acts, u_ref)
    total = jnp.zeros((256, QUERIES), jnp.float32)
    mine_ref[...] = add_blocks(
        home, plan, held, acts, u_ref, qu_ref, ids_ref, q_acts, total, kept
    )


def late_kernel(acts, u_ref, kept, *refs):
    n_blocks = kept.shape[0]
    sent_ref, held, sems = refs[n_blocks:]
    copies = [
        pltpu.make_async_copy(ref.at[pl.ds(0, HIDDEN_SIZE)], held.at[n], sems.at[n])
        for n, ref in enumerate(refs[:n_blocks])
    ]
    for each in copies:
        each.start()
    total = jnp.zeros((256, QUERIES), jnp.float32)
    for n, each in enumerate(copies):
        each.wait()
        train_v = rotate_acts(acts[...], held[n])
        for q in range(QUERIES):
            total = add_score(
                total, q, u_ref[...], kept[n, pl.ds(q * INNER, INNER), :], train_v
            )
    sent_ref[...] = total


def score_kernel(
    choice, home_ref, acts_a, u_a, acts_b, u_b, qu_ref, ids_ref, q_acts, mine_in, sent_in, *refs
):
    count = sum(choice)
    mine_ref, sent_ref, held, acts, u_ref, sems = refs[count:]
    home = home_ref[0] == 1
    plan = fetch_blocks(home, choice, refs[:count], held, sems)
    acts[:256], acts[256:] = acts_a[...], acts_b[...]
    u_ref[:256], u_ref[256:] = u_a[...], u_b[...]
    total = jnp.concatenate([mine_in[...], sent_in[...]], axis=0)
    total = add_blocks(home, plan, held, acts, u_ref, qu_ref, ids_ref, q_acts, total)
    mine_ref[...] = total[:256]
    sent_ref[...] = total[256:]


HALF = jax.ShapeDtypeStruct((256, QUERIES), jnp.float32)


def score_cost(n):
    return pl.CostEstimate(flops=n, bytes_accessed=n, transcendentals=0)


ACTS = jax.ShapeDtypeStruct((256, HIDDEN_SIZE), jnp.bfloat16)
GRADS = jax.ShapeDtypeStruct((256, INNER), jnp.bfloat16)


def score_early(home, rows, b_out, queries, blocks):
    choice = tuple(len(options) for options in blocks)
    flat = [x for options in blocks for (x,) in options]
    n = len(blocks)
    return pl.pallas_call(
        functools.partial(early_kernel, choice),
        out_shape=[
            HALF,
            ACTS,
            GRADS,
            jax.ShapeDtypeStruct((n, QUERIES * INNER, 256), jnp.bfloat16),
        ],
        in_specs=[SMEM] + [VMEM] * 5 + [ANY] * len(flat),
        out_specs=[VMEM] * 4,
        scratch_shapes=[
            pltpu.VMEM((n, HIDDEN_SIZE + INNER, 256), jnp.bfloat16),
            pltpu.SemaphoreType.DMA((n,)),
        ],
        compiler_params=pltpu.CompilerParams(vmem_limit_bytes=28 << 20),
        cost_estimate=score_cost(n),
    )(home, rows, b_out, *queries, *flat)


def score_late(acts, u, kept, blocks):
    n = len(blocks)
    return pl.pallas_call(
        late_kernel,
        out_shape=HALF,
        in_specs=[VMEM] * 3 + [ANY] * n,
        out_specs=VMEM,
        scratch_shapes=[
            pltpu.VMEM((n, HIDDEN_SIZE, 256), jnp.bfloat16),
            pltpu.SemaphoreType.DMA((n,)),
        ],
        compiler_params=pltpu.CompilerParams(vmem_limit_bytes=24 << 20),
        cost_estimate=score_cost(n),
    )(acts, u, kept, *blocks)


def score(home, rows, queries, mine_sum, sent, blocks):
    choice = tuple(len(options) for options in blocks)
    flat = [x for options in blocks for (x,) in options]
    n = len(blocks)
    return pl.pallas_call(
        functools.partial(score_kernel, choice),
        out_shape=[HALF, HALF],
        in_specs=[SMEM] + [VMEM] * 9 + [ANY] * len(flat),
        out_specs=[VMEM] * 2,
        scratch_shapes=[
            pltpu.VMEM((n, HIDDEN_SIZE + INNER, 256), jnp.bfloat16),
            pltpu.VMEM((512, HIDDEN_SIZE), jnp.bfloat16),
            pltpu.VMEM((512, INNER), jnp.bfloat16),
            pltpu.SemaphoreType.DMA((n,)),
        ],
        compiler_params=pltpu.CompilerParams(vmem_limit_bytes=24 << 20),
        cost_estimate=score_cost(n),
    )(home, *rows, *queries, mine_sum, sent, *flat)


def on_device(
    train_acts,
    train_grads,
    slot_counts,
    query_acts,
    query_grads,
    query_ids,
    basis_in,
    eigen_vals,
    basis_out,
):
    core, xl, y = lax.axis_index("core"), lax.axis_index("xl"), lax.axis_index("y")
    turn = y // 2
    is_home = core == xl
    home = is_home.astype(jnp.int32).reshape(1)
    groups = route_groups()

    turn_ref = turn.astype(jnp.int32).reshape(1)
    far = pack_block(1 - turn_ref, basis_in, eigen_vals, turn_ref)
    first = send(far, outer_step, cross_step)
    token = other_core(far[:8])
    own = pack_block(turn_ref, basis_in, eigen_vals, token)
    second = send(own, inner_step, cross_step)
    rows = pack_rows(train_acts, train_grads, far)
    rows, own = lax.optimization_barrier((rows, own))
    mine = lax.all_to_all(rows, AXES, 0, 0, axis_index_groups=groups, tiled=True)
    third = send(first, inner_step, outer_step)
    fifth = send(third, None, inner_step)
    q_own, b_own = pack_query(turn_ref, query_ids, query_acts, query_grads, basis_out, first)
    q_acts, b_out, qu, ids = query(home, q_own, other_core(q_own), b_own, other_core(b_own))
    held_second, qu = lax.optimization_barrier((second, qu))
    fourth = send(held_second, None, inner_step)
    queries = (qu, ids, q_acts)
    mine_sum, acts_a, u_a, kept = score_early(
        home, mine, b_out, queries, [[(second,)], [(third,)]]
    )
    acts_a, u_a, fourth = lax.optimization_barrier((acts_a, u_a, fourth))
    acts_b, u_b = other_core(acts_a), other_core(u_a)
    sent = score_late(acts_b, u_b, kept, [second, third])
    rows = (acts_a, u_a, acts_b, u_b)
    for blocks in ([[(own,), (fourth,)]], [[(first,), (fifth,)]]):
        mine_sum, sent = score(home, rows, queries, mine_sum, sent, blocks)
    mine_sum = mine_sum + other_core(sent)
    back = lax.all_to_all(
        mine_sum.reshape(64, SLOTS, QUERIES), AXES, 0, 0, axis_index_groups=groups, tiled=True
    )
    counts = slot_counts[0].reshape(64)
    live = jnp.arange(SLOTS)[None, :] < counts[:, None]
    return jnp.where(live[:, :, None], back, 0.0).reshape(256, QUERIES).T


def solution(mesh):
    grid = Mesh(mesh.devices.reshape(SIZES), AXES)
    expert, shard = ("xh", "z", "core"), ("xl", "y")
    whole = expert + shard
    in_specs = (
        P(whole, None),
        P(whole, None),
        P(whole, None, None),
        P(None, expert, None, None),
        P(None, expert, None, None),
        P(None, expert, None),
        P(None, expert, None, shard),
        P(None, expert, None, shard),
        P(None, expert, None, None),
    )
    return jax.shard_map(
        on_device, mesh=grid, in_specs=in_specs, out_specs=P(None, whole), check_vma=False
    )
```

```python
import functools
import math

import jax
import jax.numpy as jnp
from jax import lax
from jax.experimental import pallas as pl
from jax.experimental.pallas import tpu as pltpu
from jax.sharding import Mesh, PartitionSpec as P

HIDDEN_SIZE = 2048
INNER = 768
QUERIES = 8
SLOTS = 4
TURNS = 2
DAMPING = 0.05

SIZES = (2, 8, 2, 2, 4)
AXES = ("xh", "z", "core", "xl", "y")


def flat_index(xh, z, core, xl, y):
    return (((xh * 8 + z) * 2 + core) * 2 + xl) * 4 + y


def route_groups():
    groups = []
    for core in range(2):
        for low in range(2):
            turn_y = (low, 3 - low)
            groups.append(
                [
                    flat_index(xh, z, core, xl, turn_y[k])
                    for k in range(2)
                    for xh in range(2)
                    for z in range(8)
                    for xl in range(2)
                ]
            )
    return groups


def moves(home_step, guest_step):
    pairs = []
    for core in range(2):
        for xl in range(2):
            for y in range(4):
                step = home_step if core == xl else guest_step
                if step is not None:
                    pairs.append(((core * 2 + xl) * 4 + y, step(core, xl, y)))
    return pairs


def place(core, xl, y):
    return (core * 2 + xl) * 4 + y


def cross_step(core, xl, y):
    return place(1 - core, 1 - xl, y)


def outer_step(core, xl, y):
    return place(core, xl, 3 - y)


def inner_step(core, xl, y):
    return place(core, xl, y ^ 1)


def send(x, home_step, guest_step):
    return lax.ppermute(x, ("core", "xl", "y"), moves(home_step, guest_step))


def other_core(x):
    return lax.ppermute(x, "core", [(0, 1), (1, 0)])


def load(pairs, sems):
    copies = [
        pltpu.make_async_copy(src, dst, sems.at[n]) for n, (src, dst) in enumerate(pairs)
    ]
    for each in copies:
        each.start()
    for each in copies:
        each.wait()


def through(chunks, sems):
    inward = [
        pltpu.make_async_copy(src, mid, sems.at[0, n]) for n, (src, mid, _) in enumerate(chunks)
    ]
    outward = [
        pltpu.make_async_copy(mid, dst, sems.at[1, n]) for n, (_, mid, dst) in enumerate(chunks)
    ]
    for each in inward:
        each.start()
    for before, after in zip(inward, outward):
        before.wait()
        after.start()
    for each in outward:
        each.wait()


def block_kernel(which_ref, basis, eigen, after, block, held, sems):
    which = which_ref[0]
    chunks = []
    for start in range(0, HIDDEN_SIZE, 512):
        span = pl.ds(start, 512)
        chunks.append((basis.at[which, 0, span], held.at[span], block.at[span]))
    span = pl.ds(HIDDEN_SIZE, INNER)
    chunks.append((eigen.at[which, 0], held.at[span], block.at[span]))
    through(chunks, sems)


def query_pack_kernel(
    turn_ref, ids, q_acts, q_grads, b_out, after, q_pack, b_pack, q_held, b_held, sems
):
    turn = turn_ref[0]
    id_row = jnp.where(turn == 0, ids[0], ids[1]).astype(jnp.float32)
    b_held[INNER + 64 :, :] = jnp.zeros((16, INNER), jnp.bfloat16)
    b_held[INNER + 64 :, :64] = jnp.broadcast_to(id_row, (16, 64)).astype(jnp.bfloat16)
    load(
        [
            (q_acts.at[turn, 0], q_held),
            (b_out.at[turn, 0], b_held.at[pl.ds(0, INNER)]),
            (q_grads.at[turn, 0], b_held.at[pl.ds(INNER, 64)]),
        ],
        sems,
    )
    load([(q_held, q_pack), (b_held, b_pack)], sems)


def rows_kernel(acts, grads, after, rows):
    rows[:, :, :HIDDEN_SIZE] = acts[...].reshape(64, SLOTS, HIDDEN_SIZE)
    rows[:, :, HIDDEN_SIZE:] = grads[...].reshape(64, SLOTS, INNER)


VMEM = pl.BlockSpec(memory_space=pltpu.VMEM)
HBM = pl.BlockSpec(memory_space=pltpu.HBM)
ANY = pl.BlockSpec(memory_space=pl.ANY)
SMEM = pl.BlockSpec(memory_space=pltpu.SMEM)
BLOCK = jax.ShapeDtypeStruct((HIDDEN_SIZE + INNER, 256), jnp.bfloat16)


def pack_block(which, basis, eigen, after):
    return pl.pallas_call(
        block_kernel,
        out_shape=BLOCK,
        in_specs=[SMEM, HBM, HBM, ANY],
        out_specs=HBM,
        scratch_shapes=[pltpu.VMEM(BLOCK.shape, BLOCK.dtype), pltpu.SemaphoreType.DMA((2, 5))],
        compiler_params=pltpu.CompilerParams(vmem_limit_bytes=60 << 20),
    )(which, basis, eigen, after)


def pack_query(turn, ids, q_acts, q_grads, b_out, after):
    return pl.pallas_call(
        query_pack_kernel,
        out_shape=[
            jax.ShapeDtypeStruct((64, HIDDEN_SIZE), jnp.bfloat16),
            jax.ShapeDtypeStruct((INNER + 80, INNER), jnp.bfloat16),
        ],
        in_specs=[SMEM, VMEM] + [HBM] * 3 + [ANY],
        out_specs=[ANY] * 2,
        scratch_shapes=[
            pltpu.VMEM((64, HIDDEN_SIZE), jnp.bfloat16),
            pltpu.VMEM((INNER + 80, INNER), jnp.bfloat16),
            pltpu.SemaphoreType.DMA((3,)),
        ],
        compiler_params=pltpu.CompilerParams(vmem_limit_bytes=60 << 20),
    )(turn, ids, q_acts, q_grads, b_out, after)


def pack_rows(acts, grads, after):
    return pl.pallas_call(
        rows_kernel,
        out_shape=jax.ShapeDtypeStruct((64, SLOTS, HIDDEN_SIZE + INNER), jnp.bfloat16),
        in_specs=[VMEM, VMEM, ANY],
        out_specs=VMEM,
        compiler_params=pltpu.CompilerParams(vmem_limit_bytes=60 << 20),
    )(acts, grads, after)


def query_kernel(
    home_ref, q_own, q_other, b_own, b_other, q_acts, b_out, qu_ref, ids_ref, b_pack, sems
):
    home = home_ref[0] == 1
    options = [((b, b_pack), (q, q_acts)) for q, b in ((q_own, b_own), (q_other, b_other))]
    each_option(home, options, lambda pairs: load(pairs, sems))
    b_out[...] = b_pack[:INNER, :]
    rotated = jnp.dot(
        b_pack[INNER : INNER + 64, :], b_out[...], preferred_element_type=jnp.float32
    )
    turned = jnp.concatenate([rotated, jnp.zeros_like(rotated)], axis=0).T
    qu_ref[...] = turned[:, :64].astype(jnp.bfloat16)
    ids = b_pack[INNER + 64 : INNER + 80, :].astype(jnp.float32)[:1, :128]
    ids_ref[...] = jnp.broadcast_to(ids, (128, 128)).T[:64, :]


def query(home, q_own, q_other, b_own, b_other):
    bf16 = jnp.bfloat16
    return pl.pallas_call(
        query_kernel,
        out_shape=[
            jax.ShapeDtypeStruct((64, HIDDEN_SIZE), bf16),
            jax.ShapeDtypeStruct((INNER, INNER), bf16),
            jax.ShapeDtypeStruct((INNER, 64), bf16),
            jax.ShapeDtypeStruct((64, 128), jnp.float32),
        ],
        in_specs=[SMEM] + [ANY] * 4,
        out_specs=[VMEM] * 4,
        scratch_shapes=[
            pltpu.VMEM((INNER + 80, INNER), bf16),
            pltpu.SemaphoreType.DMA((2,)),
        ],
        compiler_params=pltpu.CompilerParams(vmem_limit_bytes=24 << 20),
        cost_estimate=pl.CostEstimate(
            flops=2 * 64 * INNER * INNER, bytes_accessed=5 << 20, transcendentals=0
        ),
    )(home, q_own, q_other, b_own, b_other)


def each_option(home, options, act):
    if len(options) == 1:
        act(options[0])
    else:
        pl.when(home)(lambda: act(options[0]))
        pl.when(jnp.logical_not(home))(lambda: act(options[1]))


PARTS = [(HIDDEN_SIZE, INNER)] + [(start, 512) for start in range(0, HIDDEN_SIZE, 512)]


def start_all(copies):
    for each in copies:
        each.start()


def fetch_blocks(home, choice, refs, held, sems):
    plan, at = [], 0
    for n, count in enumerate(choice):
        plan.append(
            [
                [
                    pltpu.make_async_copy(
                        ref.at[pl.ds(*part)], held.at[n, pl.ds(*part)], sems.at[n, m]
                    )
                    for m, part in enumerate(PARTS)
                ]
                for ref in refs[at : at + count]
            ]
        )
        each_option(home, plan[n], start_all)
        at += count
    return plan


def block_weight(held, n):
    norm_scale = 1.0 / math.sqrt(INNER * HIDDEN_SIZE)
    return norm_scale / (held[n, HIDDEN_SIZE:, :].astype(jnp.float32) + DAMPING)


def rounded(x):
    return x.astype(jnp.bfloat16).astype(jnp.float32)


def rotate_acts(acts, basis):
    return rounded(jnp.dot(acts, basis, preferred_element_type=jnp.float32))


def precondition(qu_ref, ids_ref, query_v, weight, q):
    chosen_v = jnp.where(ids_ref[:, :1] == q, query_v, 0.0).astype(jnp.bfloat16)
    rotated = jnp.dot(qu_ref[...], chosen_v, preferred_element_type=jnp.float32)
    return (rotated * weight).astype(jnp.bfloat16)


def add_score(total, q, u, precond, train_v):
    lanes = lax.broadcasted_iota(jnp.int32, total.shape, 1)
    project = jnp.dot(u, precond, preferred_element_type=jnp.float32)
    score = jnp.sum(project * train_v, axis=1, keepdims=True)
    return total + jnp.where(lanes == q, score, 0.0)


def add_blocks(home, plan, held, acts, u_ref, qu_ref, ids_ref, q_acts, total, kept=None):
    for n, options in enumerate(plan):
        each_option(home, options, lambda copies: copies[0].wait())
        weight = block_weight(held, n)
        query_v, train_v = 0.0, 0.0
        for m, part in enumerate(PARTS[1:]):
            each_option(home, options, lambda copies: copies[m + 1].wait())
            basis = held[n, pl.ds(*part), :]
            query_v += jnp.dot(
                q_acts[:, pl.ds(*part)], basis, preferred_element_type=jnp.float32
            )
            train_v += jnp.dot(acts[:, pl.ds(*part)], basis, preferred_element_type=jnp.float32)
        train_v = rounded(train_v)
        for q in range(QUERIES):
            precond = precondition(qu_ref, ids_ref, query_v, weight, q)
            if kept is not None:
                kept[n, pl.ds(q * INNER, INNER), :] = precond
            total = add_score(total, q, u_ref[...], precond, train_v)
    return total


def unpack_rows(rows, b_out, acts, u_ref):
    acts[...] = rows[:, :, :HIDDEN_SIZE].reshape(256, HIDDEN_SIZE)
    u_ref[...] = jnp.dot(
        rows[:, :, HIDDEN_SIZE:].reshape(256, INNER),
        b_out[...],
        preferred_element_type=jnp.float32,
    ).astype(jnp.bfloat16)


def early_kernel(choice, home_ref, rows, b_out, qu_ref, ids_ref, q_acts, *refs):
    count = sum(choice)
    mine_ref, acts, u_ref, kept, held, sems = refs[count:]
    home = home_ref[0] == 1
    plan = fetch_blocks(home, choice, refs[:count], held, sems)
    unpack_rows(rows, b_out, acts, u_ref)
    total = jnp.zeros((256, QUERIES), jnp.float32)
    mine_ref[...] = add_blocks(
        home, plan, held, acts, u_ref, qu_ref, ids_ref, q_acts, total, kept
    )


def late_kernel(acts_a, u_a, acts, u_ref, kept, *refs):
    n_blocks = kept.shape[0]
    sent_ref, acts_all, u_all, held, sems = refs[n_blocks:]
    copies = [
        pltpu.make_async_copy(ref.at[pl.ds(0, HIDDEN_SIZE)], held.at[n], sems.at[n])
        for n, ref in enumerate(refs[:n_blocks])
    ]
    for each in copies:
        each.start()
    acts_all[:256], acts_all[256:] = acts_a[...], acts[...]
    u_all[:256], u_all[256:] = u_a[...], u_ref[...]
    total = jnp.zeros((256, QUERIES), jnp.float32)
    for n, each in enumerate(copies):
        each.wait()
        train_v = rotate_acts(acts[...], held[n])
        for q in range(QUERIES):
            total = add_score(
                total, q, u_ref[...], kept[n, pl.ds(q * INNER, INNER), :], train_v
            )
    sent_ref[...] = total


def score_kernel(
    choice, home_ref, acts, u_ref, qu_ref, ids_ref, q_acts, mine_in, sent_in, *refs
):
    count = sum(choice)
    mine_ref, sent_ref, held, sems = refs[count:]
    home = home_ref[0] == 1
    plan = fetch_blocks(home, choice, refs[:count], held, sems)
    total = jnp.concatenate([mine_in[...], sent_in[...]], axis=0)
    total = add_blocks(home, plan, held, acts, u_ref, qu_ref, ids_ref, q_acts, total)
    mine_ref[...] = total[:256]
    sent_ref[...] = total[256:]


HALF = jax.ShapeDtypeStruct((256, QUERIES), jnp.float32)


def score_cost(n):
    return pl.CostEstimate(flops=n, bytes_accessed=n, transcendentals=0)


ACTS = jax.ShapeDtypeStruct((256, HIDDEN_SIZE), jnp.bfloat16)
GRADS = jax.ShapeDtypeStruct((256, INNER), jnp.bfloat16)


def score_early(home, rows, b_out, queries, blocks):
    choice = tuple(len(options) for options in blocks)
    flat = [x for options in blocks for (x,) in options]
    n = len(blocks)
    return pl.pallas_call(
        functools.partial(early_kernel, choice),
        out_shape=[
            HALF,
            ACTS,
            GRADS,
            jax.ShapeDtypeStruct((n, QUERIES * INNER, 256), jnp.bfloat16),
        ],
        in_specs=[SMEM] + [VMEM] * 5 + [ANY] * len(flat),
        out_specs=[VMEM] * 4,
        scratch_shapes=[
            pltpu.VMEM((n, HIDDEN_SIZE + INNER, 256), jnp.bfloat16),
            pltpu.SemaphoreType.DMA((n, len(PARTS))),
        ],
        compiler_params=pltpu.CompilerParams(vmem_limit_bytes=28 << 20),
        cost_estimate=score_cost(n),
    )(home, rows, b_out, *queries, *flat)


def score_late(acts_a, u_a, acts_b, u_b, kept, blocks):
    n = len(blocks)
    return pl.pallas_call(
        late_kernel,
        out_shape=[
            HALF,
            jax.ShapeDtypeStruct((512, HIDDEN_SIZE), jnp.bfloat16),
            jax.ShapeDtypeStruct((512, INNER), jnp.bfloat16),
        ],
        in_specs=[VMEM] * 5 + [ANY] * n,
        out_specs=[VMEM] * 3,
        scratch_shapes=[
            pltpu.VMEM((n, HIDDEN_SIZE, 256), jnp.bfloat16),
            pltpu.SemaphoreType.DMA((n,)),
        ],
        compiler_params=pltpu.CompilerParams(vmem_limit_bytes=24 << 20),
        cost_estimate=score_cost(n),
    )(acts_a, u_a, acts_b, u_b, kept, *blocks)


def score(home, rows, queries, mine_sum, sent, blocks):
    choice = tuple(len(options) for options in blocks)
    flat = [x for options in blocks for (x,) in options]
    n = len(blocks)
    return pl.pallas_call(
        functools.partial(score_kernel, choice),
        out_shape=[HALF, HALF],
        in_specs=[SMEM] + [VMEM] * 7 + [ANY] * len(flat),
        out_specs=[VMEM] * 2,
        scratch_shapes=[
            pltpu.VMEM((n, HIDDEN_SIZE + INNER, 256), jnp.bfloat16),
            pltpu.SemaphoreType.DMA((n, len(PARTS))),
        ],
        compiler_params=pltpu.CompilerParams(vmem_limit_bytes=24 << 20),
        cost_estimate=score_cost(n),
    )(home, *rows, *queries, mine_sum, sent, *flat)


def on_device(
    train_acts,
    train_grads,
    slot_counts,
    query_acts,
    query_grads,
    query_ids,
    basis_in,
    eigen_vals,
    basis_out,
):
    core, xl, y = lax.axis_index("core"), lax.axis_index("xl"), lax.axis_index("y")
    turn = y // 2
    is_home = core == xl
    home = is_home.astype(jnp.int32).reshape(1)
    groups = route_groups()

    turn_ref = turn.astype(jnp.int32).reshape(1)
    far = pack_block(1 - turn_ref, basis_in, eigen_vals, turn_ref)
    first = send(far, outer_step, cross_step)
    token = other_core(far[:8])
    own = pack_block(turn_ref, basis_in, eigen_vals, token)
    second = send(own, inner_step, cross_step)
    rows = pack_rows(train_acts, train_grads, far)
    rows, own = lax.optimization_barrier((rows, own))
    mine = lax.all_to_all(rows, AXES, 0, 0, axis_index_groups=groups, tiled=True)
    third = send(first, inner_step, outer_step)
    fifth = send(third, None, inner_step)
    q_own, b_own = pack_query(turn_ref, query_ids, query_acts, query_grads, basis_out, first)
    q_acts, b_out, qu, ids = query(home, q_own, other_core(q_own), b_own, other_core(b_own))
    held_second, qu = lax.optimization_barrier((second, qu))
    fourth = send(held_second, None, inner_step)
    queries = (qu, ids, q_acts)
    mine_sum, acts_a, u_a, kept = score_early(
        home, mine, b_out, queries, [[(second,)], [(third,)]]
    )
    acts_a, u_a, fourth = lax.optimization_barrier((acts_a, u_a, fourth))
    acts_b, u_b = other_core(acts_a), other_core(u_a)
    sent, acts, u = score_late(acts_a, u_a, acts_b, u_b, kept, [second, third])
    rows = (acts, u)
    for blocks in ([[(own,), (fourth,)]], [[(first,), (fifth,)]]):
        mine_sum, sent = score(home, rows, queries, mine_sum, sent, blocks)
    mine_sum = mine_sum + other_core(sent)
    back = lax.all_to_all(
        mine_sum.reshape(64, SLOTS, QUERIES), AXES, 0, 0, axis_index_groups=groups, tiled=True
    )
    counts = slot_counts[0].reshape(64)
    live = jnp.arange(SLOTS)[None, :] < counts[:, None]
    return jnp.where(live[:, :, None], back, 0.0).reshape(256, QUERIES).T


def solution(mesh):
    grid = Mesh(mesh.devices.reshape(SIZES), AXES)
    expert, shard = ("xh", "z", "core"), ("xl", "y")
    whole = expert + shard
    in_specs = (
        P(whole, None),
        P(whole, None),
        P(whole, None, None),
        P(None, expert, None, None),
        P(None, expert, None, None),
        P(None, expert, None),
        P(None, expert, None, shard),
        P(None, expert, None, shard),
        P(None, expert, None, None),
    )
    return jax.shard_map(
        on_device, mesh=grid, in_specs=in_specs, out_specs=P(None, whole), check_vma=False
    )
```

```python
import functools
import math

import jax
import jax.numpy as jnp
from jax import lax
from jax.experimental import pallas as pl
from jax.experimental.pallas import tpu as pltpu
from jax.sharding import Mesh, PartitionSpec as P

HIDDEN_SIZE = 2048
INNER = 768
QUERIES = 8
SLOTS = 4
TURNS = 2
DAMPING = 0.05

SIZES = (2, 8, 2, 2, 4)
AXES = ("xh", "z", "core", "xl", "y")


def flat_index(xh, z, core, xl, y):
    return (((xh * 8 + z) * 2 + core) * 2 + xl) * 4 + y


def route_groups():
    groups = []
    for core in range(2):
        for low in range(2):
            turn_y = (low, 3 - low)
            groups.append(
                [
                    flat_index(xh, z, core, xl, turn_y[k])
                    for k in range(2)
                    for xh in range(2)
                    for z in range(8)
                    for xl in range(2)
                ]
            )
    return groups


def return_groups():
    return [
        [
            flat_index(xh, z, core, xl, (low, 3 - low)[k])
            for core in range(2)
            for k in range(2)
            for xh in range(2)
            for z in range(8)
            for xl in range(2)
        ]
        for low in range(2)
    ]


def moves(home_step, guest_step):
    pairs = []
    for core in range(2):
        for xl in range(2):
            for y in range(4):
                step = home_step if core == xl else guest_step
                if step is not None:
                    pairs.append(((core * 2 + xl) * 4 + y, step(core, xl, y)))
    return pairs


def place(core, xl, y):
    return (core * 2 + xl) * 4 + y


def cross_step(core, xl, y):
    return place(1 - core, 1 - xl, y)


def outer_step(core, xl, y):
    return place(core, xl, 3 - y)


def inner_step(core, xl, y):
    return place(core, xl, y ^ 1)


def send(x, home_step, guest_step):
    return lax.ppermute(x, ("core", "xl", "y"), moves(home_step, guest_step))


def other_core(x):
    return lax.ppermute(x, "core", [(0, 1), (1, 0)])


def load(pairs, sems):
    copies = [
        pltpu.make_async_copy(src, dst, sems.at[n]) for n, (src, dst) in enumerate(pairs)
    ]
    for each in copies:
        each.start()
    for each in copies:
        each.wait()


def through(chunks, sems):
    inward = [
        pltpu.make_async_copy(src, mid, sems.at[0, n]) for n, (src, mid, _) in enumerate(chunks)
    ]
    outward = [
        pltpu.make_async_copy(mid, dst, sems.at[1, n]) for n, (_, mid, dst) in enumerate(chunks)
    ]
    for each in inward:
        each.start()
    for before, after in zip(inward, outward):
        before.wait()
        after.start()
    for each in outward:
        each.wait()


def block_kernel(which_ref, basis, eigen, after, block, held, sems):
    which = which_ref[0]
    chunks = []
    for start in range(0, HIDDEN_SIZE, 512):
        span = pl.ds(start, 512)
        chunks.append((basis.at[which, 0, span], held.at[span], block.at[span]))
    span = pl.ds(HIDDEN_SIZE, INNER)
    chunks.append((eigen.at[which, 0], held.at[span], block.at[span]))
    through(chunks, sems)


def query_pack_kernel(
    turn_ref, ids, q_acts, q_grads, b_out, after, q_pack, b_pack, q_held, b_held, sems
):
    turn = turn_ref[0]
    id_row = jnp.where(turn == 0, ids[0], ids[1]).astype(jnp.float32)
    b_held[INNER + 64 :, :] = jnp.zeros((16, INNER), jnp.bfloat16)
    b_held[INNER + 64 :, :64] = jnp.broadcast_to(id_row, (16, 64)).astype(jnp.bfloat16)
    load(
        [
            (q_acts.at[turn, 0], q_held),
            (b_out.at[turn, 0], b_held.at[pl.ds(0, INNER)]),
            (q_grads.at[turn, 0], b_held.at[pl.ds(INNER, 64)]),
        ],
        sems,
    )
    load([(q_held, q_pack), (b_held, b_pack)], sems)


def rows_kernel(acts, grads, after, rows):
    rows[:, :, :HIDDEN_SIZE] = acts[...].reshape(64, SLOTS, HIDDEN_SIZE)
    rows[:, :, HIDDEN_SIZE:] = grads[...].reshape(64, SLOTS, INNER)


VMEM = pl.BlockSpec(memory_space=pltpu.VMEM)
HBM = pl.BlockSpec(memory_space=pltpu.HBM)
ANY = pl.BlockSpec(memory_space=pl.ANY)
SMEM = pl.BlockSpec(memory_space=pltpu.SMEM)
BLOCK = jax.ShapeDtypeStruct((HIDDEN_SIZE + INNER, 256), jnp.bfloat16)


def pack_block(which, basis, eigen, after):
    return pl.pallas_call(
        block_kernel,
        out_shape=BLOCK,
        in_specs=[SMEM, HBM, HBM, ANY],
        out_specs=HBM,
        scratch_shapes=[pltpu.VMEM(BLOCK.shape, BLOCK.dtype), pltpu.SemaphoreType.DMA((2, 5))],
        compiler_params=pltpu.CompilerParams(vmem_limit_bytes=60 << 20),
    )(which, basis, eigen, after)


def pack_query(turn, ids, q_acts, q_grads, b_out, after):
    return pl.pallas_call(
        query_pack_kernel,
        out_shape=[
            jax.ShapeDtypeStruct((64, HIDDEN_SIZE), jnp.bfloat16),
            jax.ShapeDtypeStruct((INNER + 80, INNER), jnp.bfloat16),
        ],
        in_specs=[SMEM, VMEM] + [HBM] * 3 + [ANY],
        out_specs=[ANY] * 2,
        scratch_shapes=[
            pltpu.VMEM((64, HIDDEN_SIZE), jnp.bfloat16),
            pltpu.VMEM((INNER + 80, INNER), jnp.bfloat16),
            pltpu.SemaphoreType.DMA((3,)),
        ],
        compiler_params=pltpu.CompilerParams(vmem_limit_bytes=60 << 20),
    )(turn, ids, q_acts, q_grads, b_out, after)


def pack_rows(acts, grads, after):
    return pl.pallas_call(
        rows_kernel,
        out_shape=jax.ShapeDtypeStruct((64, SLOTS, HIDDEN_SIZE + INNER), jnp.bfloat16),
        in_specs=[VMEM, VMEM, ANY],
        out_specs=VMEM,
        compiler_params=pltpu.CompilerParams(vmem_limit_bytes=60 << 20),
    )(acts, grads, after)


def query_kernel(
    home_ref, q_own, q_other, b_own, b_other, q_acts, b_out, qu_ref, ids_ref, b_pack, sems
):
    home = home_ref[0] == 1
    options = [((b, b_pack), (q, q_acts)) for q, b in ((q_own, b_own), (q_other, b_other))]
    each_option(home, options, lambda pairs: load(pairs, sems))
    b_out[...] = b_pack[:INNER, :]
    rotated = jnp.dot(
        b_pack[INNER : INNER + 64, :], b_out[...], preferred_element_type=jnp.float32
    )
    turned = jnp.concatenate([rotated, jnp.zeros_like(rotated)], axis=0).T
    qu_ref[...] = turned[:, :64].astype(jnp.bfloat16)
    ids = b_pack[INNER + 64 : INNER + 80, :].astype(jnp.float32)[:1, :128]
    ids_ref[...] = jnp.broadcast_to(ids, (128, 128)).T[:64, :]


def query(home, q_own, q_other, b_own, b_other):
    bf16 = jnp.bfloat16
    return pl.pallas_call(
        query_kernel,
        out_shape=[
            jax.ShapeDtypeStruct((64, HIDDEN_SIZE), bf16),
            jax.ShapeDtypeStruct((INNER, INNER), bf16),
            jax.ShapeDtypeStruct((INNER, 64), bf16),
            jax.ShapeDtypeStruct((64, 128), jnp.float32),
        ],
        in_specs=[SMEM] + [ANY] * 4,
        out_specs=[VMEM] * 4,
        scratch_shapes=[
            pltpu.VMEM((INNER + 80, INNER), bf16),
            pltpu.SemaphoreType.DMA((2,)),
        ],
        compiler_params=pltpu.CompilerParams(vmem_limit_bytes=24 << 20),
        cost_estimate=pl.CostEstimate(
            flops=2 * 64 * INNER * INNER, bytes_accessed=5 << 20, transcendentals=0
        ),
    )(home, q_own, q_other, b_own, b_other)


def each_option(home, options, act):
    if len(options) == 1:
        act(options[0])
    else:
        pl.when(home)(lambda: act(options[0]))
        pl.when(jnp.logical_not(home))(lambda: act(options[1]))


def fetch_blocks(home, choice, refs, held, sems):
    plan, at = [], 0
    for n, count in enumerate(choice):
        plan.append(
            [pltpu.make_async_copy(ref, held.at[n], sems.at[n]) for ref in refs[at : at + count]]
        )
        each_option(home, plan[n], lambda copy: copy.start())
        at += count
    return plan


def block_weight(held, n):
    norm_scale = 1.0 / math.sqrt(INNER * HIDDEN_SIZE)
    return norm_scale / (held[n, HIDDEN_SIZE:, :].astype(jnp.float32) + DAMPING)


def rotate_acts(acts, basis):
    train_v = jnp.dot(acts, basis, preferred_element_type=jnp.float32)
    return train_v.astype(jnp.bfloat16).astype(jnp.float32)


def precondition(qu_ref, ids_ref, query_v, weight, q):
    chosen_v = jnp.where(ids_ref[:, :1] == q, query_v, 0.0).astype(jnp.bfloat16)
    rotated = jnp.dot(qu_ref[...], chosen_v, preferred_element_type=jnp.float32)
    return (rotated * weight).astype(jnp.bfloat16)


def add_score(total, q, u, precond, train_v):
    lanes = lax.broadcasted_iota(jnp.int32, total.shape, 1)
    project = jnp.dot(u, precond, preferred_element_type=jnp.float32)
    score = jnp.sum(project * train_v, axis=1, keepdims=True)
    return total + jnp.where(lanes == q, score, 0.0)


def add_blocks(home, plan, held, acts, u_ref, qu_ref, ids_ref, q_acts, total, kept=None):
    for n, options in enumerate(plan):
        each_option(home, options, lambda copy: copy.wait())
        basis = held[n, :HIDDEN_SIZE, :]
        weight = block_weight(held, n)
        query_v = jnp.dot(q_acts[...], basis, preferred_element_type=jnp.float32)
        train_v = rotate_acts(acts[...], basis)
        for q in range(QUERIES):
            precond = precondition(qu_ref, ids_ref, query_v, weight, q)
            if kept is not None:
                kept[n, pl.ds(q * INNER, INNER), :] = precond
            total = add_score(total, q, u_ref[...], precond, train_v)
    return total


def unpack_rows(rows, b_out, acts, u_ref):
    acts[...] = rows[:, :, :HIDDEN_SIZE].reshape(256, HIDDEN_SIZE)
    u_ref[...] = jnp.dot(
        rows[:, :, HIDDEN_SIZE:].reshape(256, INNER),
        b_out[...],
        preferred_element_type=jnp.float32,
    ).astype(jnp.bfloat16)


def early_kernel(choice, home_ref, rows, b_out, qu_ref, ids_ref, q_acts, *refs):
    count = sum(choice)
    mine_ref, acts, u_ref, kept, held, sems = refs[count:]
    home = home_ref[0] == 1
    plan = fetch_blocks(home, choice, refs[:count], held, sems)
    unpack_rows(rows, b_out, acts, u_ref)
    total = jnp.zeros((256, QUERIES), jnp.float32)
    mine_ref[...] = add_blocks(
        home, plan, held, acts, u_ref, qu_ref, ids_ref, q_acts, total, kept
    )


def late_kernel(acts_a, u_a, acts, u_ref, kept, *refs):
    n_blocks = kept.shape[0]
    sent_ref, acts_all, u_all, held, sems = refs[n_blocks:]
    copies = [
        pltpu.make_async_copy(ref.at[pl.ds(0, HIDDEN_SIZE)], held.at[n], sems.at[n])
        for n, ref in enumerate(refs[:n_blocks])
    ]
    for each in copies:
        each.start()
    acts_all[:256], acts_all[256:] = acts_a[...], acts[...]
    u_all[:256], u_all[256:] = u_a[...], u_ref[...]
    total = jnp.zeros((256, QUERIES), jnp.float32)
    for n, each in enumerate(copies):
        each.wait()
        train_v = rotate_acts(acts[...], held[n])
        for q in range(QUERIES):
            total = add_score(
                total, q, u_ref[...], kept[n, pl.ds(q * INNER, INNER), :], train_v
            )
    sent_ref[...] = total


def score_kernel(
    choice, last, home_ref, acts, u_ref, qu_ref, ids_ref, q_acts, mine_in, sent_in, *refs
):
    count = sum(choice)
    *out_refs, held, sems = refs[count:]
    home = home_ref[0] == 1
    plan = fetch_blocks(home, choice, refs[:count], held, sems)
    total = jnp.concatenate([mine_in[...], sent_in[...]], axis=0)
    total = add_blocks(home, plan, held, acts, u_ref, qu_ref, ids_ref, q_acts, total)
    if last:
        core = home_ref[1]
        out_refs[0][core] = total[:256]
        out_refs[0][1 - core] = total[256:]
    else:
        out_refs[0][...] = total[:256]
        out_refs[1][...] = total[256:]


HALF = jax.ShapeDtypeStruct((256, QUERIES), jnp.float32)
BOTH = jax.ShapeDtypeStruct((2, 256, QUERIES), jnp.float32)


def score_cost(n):
    return pl.CostEstimate(flops=n, bytes_accessed=n, transcendentals=0)


ACTS = jax.ShapeDtypeStruct((256, HIDDEN_SIZE), jnp.bfloat16)
GRADS = jax.ShapeDtypeStruct((256, INNER), jnp.bfloat16)


def score_early(home, rows, b_out, queries, blocks):
    choice = tuple(len(options) for options in blocks)
    flat = [x for options in blocks for (x,) in options]
    n = len(blocks)
    return pl.pallas_call(
        functools.partial(early_kernel, choice),
        out_shape=[
            HALF,
            ACTS,
            GRADS,
            jax.ShapeDtypeStruct((n, QUERIES * INNER, 256), jnp.bfloat16),
        ],
        in_specs=[SMEM] + [VMEM] * 5 + [ANY] * len(flat),
        out_specs=[VMEM] * 4,
        scratch_shapes=[
            pltpu.VMEM((n, HIDDEN_SIZE + INNER, 256), jnp.bfloat16),
            pltpu.SemaphoreType.DMA((n,)),
        ],
        compiler_params=pltpu.CompilerParams(vmem_limit_bytes=28 << 20),
        cost_estimate=score_cost(n),
    )(home, rows, b_out, *queries, *flat)


def score_late(acts_a, u_a, acts_b, u_b, kept, blocks):
    n = len(blocks)
    return pl.pallas_call(
        late_kernel,
        out_shape=[
            HALF,
            jax.ShapeDtypeStruct((512, HIDDEN_SIZE), jnp.bfloat16),
            jax.ShapeDtypeStruct((512, INNER), jnp.bfloat16),
        ],
        in_specs=[VMEM] * 5 + [ANY] * n,
        out_specs=[VMEM] * 3,
        scratch_shapes=[
            pltpu.VMEM((n, HIDDEN_SIZE, 256), jnp.bfloat16),
            pltpu.SemaphoreType.DMA((n,)),
        ],
        compiler_params=pltpu.CompilerParams(vmem_limit_bytes=24 << 20),
        cost_estimate=score_cost(n),
    )(acts_a, u_a, acts_b, u_b, kept, *blocks)


def score(home, rows, queries, mine_sum, sent, blocks, last):
    choice = tuple(len(options) for options in blocks)
    flat = [x for options in blocks for (x,) in options]
    n = len(blocks)
    return pl.pallas_call(
        functools.partial(score_kernel, choice, last),
        out_shape=[BOTH] if last else [HALF, HALF],
        in_specs=[SMEM] + [VMEM] * 7 + [ANY] * len(flat),
        out_specs=[VMEM] if last else [VMEM] * 2,
        scratch_shapes=[
            pltpu.VMEM((n, HIDDEN_SIZE + INNER, 256), jnp.bfloat16),
            pltpu.SemaphoreType.DMA((n,)),
        ],
        compiler_params=pltpu.CompilerParams(vmem_limit_bytes=24 << 20),
        cost_estimate=score_cost(n),
    )(home, *rows, *queries, mine_sum, sent, *flat)


def on_device(
    train_acts,
    train_grads,
    slot_counts,
    query_acts,
    query_grads,
    query_ids,
    basis_in,
    eigen_vals,
    basis_out,
):
    core, xl, y = lax.axis_index("core"), lax.axis_index("xl"), lax.axis_index("y")
    turn = y // 2
    is_home = core == xl
    home = jnp.stack([is_home.astype(jnp.int32), core.astype(jnp.int32)])
    groups = route_groups()

    turn_ref = turn.astype(jnp.int32).reshape(1)
    far = pack_block(1 - turn_ref, basis_in, eigen_vals, turn_ref)
    first = send(far, outer_step, cross_step)
    token = other_core(far[:8])
    own = pack_block(turn_ref, basis_in, eigen_vals, token)
    second = send(own, inner_step, cross_step)
    rows = pack_rows(train_acts, train_grads, far)
    rows, own = lax.optimization_barrier((rows, own))
    mine = lax.all_to_all(rows, AXES, 0, 0, axis_index_groups=groups, tiled=True)
    third = send(first, inner_step, outer_step)
    fifth = send(third, None, inner_step)
    q_own, b_own = pack_query(turn_ref, query_ids, query_acts, query_grads, basis_out, first)
    q_acts, b_out, qu, ids = query(home, q_own, other_core(q_own), b_own, other_core(b_own))
    held_second, qu = lax.optimization_barrier((second, qu))
    fourth = send(held_second, None, inner_step)
    counts = slot_counts[0].reshape(64)
    live = (jnp.arange(SLOTS)[None, :] < counts[:, None]).astype(jnp.float32)
    live, qu = lax.optimization_barrier((live, qu))
    queries = (qu, ids, q_acts)
    mine_sum, acts_a, u_a, kept = score_early(
        home, mine, b_out, queries, [[(second,)], [(third,)]]
    )
    acts_a, u_a, fourth = lax.optimization_barrier((acts_a, u_a, fourth))
    acts_b, u_b = other_core(acts_a), other_core(u_a)
    sent, acts, u = score_late(acts_a, u_a, acts_b, u_b, kept, [second, third])
    rows = (acts, u)
    mine_sum, sent = score(
        home, rows, queries, mine_sum, sent, [[(own,), (fourth,)]], False
    )
    (both,) = score(home, rows, queries, mine_sum, sent, [[(first,), (fifth,)]], True)
    back = lax.all_to_all(
        both.reshape(128, SLOTS, QUERIES),
        AXES,
        0,
        0,
        axis_index_groups=return_groups(),
        tiled=True,
    )
    back = back[:64] + back[64:]
    return jnp.where(live[:, :, None] > 0, back, 0.0).reshape(256, QUERIES).T


def solution(mesh):
    grid = Mesh(mesh.devices.reshape(SIZES), AXES)
    expert, shard = ("xh", "z", "core"), ("xl", "y")
    whole = expert + shard
    in_specs = (
        P(whole, None),
        P(whole, None),
        P(whole, None, None),
        P(None, expert, None, None),
        P(None, expert, None, None),
        P(None, expert, None),
        P(None, expert, None, shard),
        P(None, expert, None, shard),
        P(None, expert, None, None),
    )
    return jax.shard_map(
        on_device, mesh=grid, in_specs=in_specs, out_specs=P(None, whole), check_vma=False
    )
```

```python
import functools
import math

import jax
import jax.numpy as jnp
from jax import lax
from jax.experimental import pallas as pl
from jax.experimental.pallas import tpu as pltpu
from jax.sharding import Mesh, PartitionSpec as P

HIDDEN_SIZE = 2048
INNER = 768
QUERIES = 8
SLOTS = 4
TURNS = 2
DAMPING = 0.05

SIZES = (2, 8, 2, 2, 4)
AXES = ("xh", "z", "core", "xl", "y")


def flat_index(xh, z, core, xl, y):
    return (((xh * 8 + z) * 2 + core) * 2 + xl) * 4 + y


def route_groups():
    groups = []
    for core in range(2):
        for low in range(2):
            turn_y = (low, 3 - low)
            groups.append(
                [
                    flat_index(xh, z, core, xl, turn_y[k])
                    for k in range(2)
                    for xh in range(2)
                    for z in range(8)
                    for xl in range(2)
                ]
            )
    return groups


def moves(home_step, guest_step):
    pairs = []
    for core in range(2):
        for xl in range(2):
            for y in range(4):
                step = home_step if core == xl else guest_step
                if step is not None:
                    pairs.append(((core * 2 + xl) * 4 + y, step(core, xl, y)))
    return pairs


def place(core, xl, y):
    return (core * 2 + xl) * 4 + y


def cross_step(core, xl, y):
    return place(1 - core, 1 - xl, y)


def outer_step(core, xl, y):
    return place(core, xl, 3 - y)


def inner_step(core, xl, y):
    return place(core, xl, y ^ 1)


def send(x, home_step, guest_step):
    return lax.ppermute(x, ("core", "xl", "y"), moves(home_step, guest_step))


def other_core(x):
    return lax.ppermute(x, "core", [(0, 1), (1, 0)])


def load(pairs, sems):
    copies = [
        pltpu.make_async_copy(src, dst, sems.at[n]) for n, (src, dst) in enumerate(pairs)
    ]
    for each in copies:
        each.start()
    for each in copies:
        each.wait()


def through(chunks, sems):
    inward = [
        pltpu.make_async_copy(src, mid, sems.at[0, n]) for n, (src, mid, _) in enumerate(chunks)
    ]
    outward = [
        pltpu.make_async_copy(mid, dst, sems.at[1, n]) for n, (_, mid, dst) in enumerate(chunks)
    ]
    for each in inward:
        each.start()
    for before, after in zip(inward, outward):
        before.wait()
        after.start()
    for each in outward:
        each.wait()


def block_kernel(which_ref, basis, eigen, after, block, held, sems):
    which = which_ref[0]
    chunks = []
    for start in range(0, HIDDEN_SIZE, 512):
        span = pl.ds(start, 512)
        chunks.append((basis.at[which, 0, span], held.at[span], block.at[span]))
    span = pl.ds(HIDDEN_SIZE, INNER)
    chunks.append((eigen.at[which, 0], held.at[span], block.at[span]))
    through(chunks, sems)


def query_pack_kernel(
    turn_ref, ids, q_acts, q_grads, b_out, after, q_pack, b_pack, q_held, b_held, sems
):
    turn = turn_ref[0]
    id_row = jnp.where(turn == 0, ids[0], ids[1]).astype(jnp.float32)
    b_held[INNER + 64 :, :] = jnp.zeros((16, INNER), jnp.bfloat16)
    b_held[INNER + 64 :, :64] = jnp.broadcast_to(id_row, (16, 64)).astype(jnp.bfloat16)
    load(
        [
            (q_acts.at[turn, 0], q_held),
            (b_out.at[turn, 0], b_held.at[pl.ds(0, INNER)]),
            (q_grads.at[turn, 0], b_held.at[pl.ds(INNER, 64)]),
        ],
        sems,
    )
    load([(q_held, q_pack), (b_held, b_pack)], sems)


def rows_kernel(acts, grads, after, rows):
    rows[:, :, :HIDDEN_SIZE] = acts[...].reshape(64, SLOTS, HIDDEN_SIZE)
    rows[:, :, HIDDEN_SIZE:] = grads[...].reshape(64, SLOTS, INNER)


VMEM = pl.BlockSpec(memory_space=pltpu.VMEM)
HBM = pl.BlockSpec(memory_space=pltpu.HBM)
ANY = pl.BlockSpec(memory_space=pl.ANY)
SMEM = pl.BlockSpec(memory_space=pltpu.SMEM)
BLOCK = jax.ShapeDtypeStruct((HIDDEN_SIZE + INNER, 256), jnp.bfloat16)


def pack_block(which, basis, eigen, after):
    return pl.pallas_call(
        block_kernel,
        out_shape=BLOCK,
        in_specs=[SMEM, HBM, HBM, ANY],
        out_specs=HBM,
        scratch_shapes=[pltpu.VMEM(BLOCK.shape, BLOCK.dtype), pltpu.SemaphoreType.DMA((2, 5))],
        compiler_params=pltpu.CompilerParams(vmem_limit_bytes=60 << 20),
    )(which, basis, eigen, after)


def pack_query(turn, ids, q_acts, q_grads, b_out, after):
    return pl.pallas_call(
        query_pack_kernel,
        out_shape=[
            jax.ShapeDtypeStruct((64, HIDDEN_SIZE), jnp.bfloat16),
            jax.ShapeDtypeStruct((INNER + 80, INNER), jnp.bfloat16),
        ],
        in_specs=[SMEM, VMEM] + [HBM] * 3 + [ANY],
        out_specs=[ANY] * 2,
        scratch_shapes=[
            pltpu.VMEM((64, HIDDEN_SIZE), jnp.bfloat16),
            pltpu.VMEM((INNER + 80, INNER), jnp.bfloat16),
            pltpu.SemaphoreType.DMA((3,)),
        ],
        compiler_params=pltpu.CompilerParams(vmem_limit_bytes=60 << 20),
    )(turn, ids, q_acts, q_grads, b_out, after)


def pack_rows(acts, grads, after):
    return pl.pallas_call(
        rows_kernel,
        out_shape=jax.ShapeDtypeStruct((64, SLOTS, HIDDEN_SIZE + INNER), jnp.bfloat16),
        in_specs=[VMEM, VMEM, ANY],
        out_specs=VMEM,
        compiler_params=pltpu.CompilerParams(vmem_limit_bytes=60 << 20),
    )(acts, grads, after)


def query_kernel(
    home_ref, q_own, q_other, b_own, b_other, q_acts, b_out, qu_ref, ids_ref, b_pack, sems
):
    home = home_ref[0] == 1
    options = [((b, b_pack), (q, q_acts)) for q, b in ((q_own, b_own), (q_other, b_other))]
    each_option(home, options, lambda pairs: load(pairs, sems))
    b_out[...] = b_pack[:INNER, :]
    rotated = jnp.dot(
        b_pack[INNER : INNER + 64, :], b_out[...], preferred_element_type=jnp.float32
    )
    turned = jnp.concatenate([rotated, jnp.zeros_like(rotated)], axis=0).T
    qu_ref[...] = turned[:, :64].astype(jnp.bfloat16)
    ids = b_pack[INNER + 64 : INNER + 80, :].astype(jnp.float32)[:1, :128]
    ids_ref[...] = jnp.broadcast_to(ids, (128, 128)).T[:64, :]


def query(home, q_own, q_other, b_own, b_other):
    bf16 = jnp.bfloat16
    return pl.pallas_call(
        query_kernel,
        out_shape=[
            jax.ShapeDtypeStruct((64, HIDDEN_SIZE), bf16),
            jax.ShapeDtypeStruct((INNER, INNER), bf16),
            jax.ShapeDtypeStruct((INNER, 64), bf16),
            jax.ShapeDtypeStruct((64, 128), jnp.float32),
        ],
        in_specs=[SMEM] + [ANY] * 4,
        out_specs=[VMEM] * 4,
        scratch_shapes=[
            pltpu.VMEM((INNER + 80, INNER), bf16),
            pltpu.SemaphoreType.DMA((2,)),
        ],
        compiler_params=pltpu.CompilerParams(vmem_limit_bytes=24 << 20),
        cost_estimate=pl.CostEstimate(
            flops=2 * 64 * INNER * INNER, bytes_accessed=5 << 20, transcendentals=0
        ),
    )(home, q_own, q_other, b_own, b_other)


def each_option(home, options, act):
    if len(options) == 1:
        act(options[0])
    else:
        pl.when(home)(lambda: act(options[0]))
        pl.when(jnp.logical_not(home))(lambda: act(options[1]))


def fetch_blocks(home, choice, refs, held, sems):
    plan, at = [], 0
    for n, count in enumerate(choice):
        plan.append(
            [pltpu.make_async_copy(ref, held.at[n], sems.at[n]) for ref in refs[at : at + count]]
        )
        each_option(home, plan[n], lambda copy: copy.start())
        at += count
    return plan


def block_weight(held, n):
    norm_scale = 1.0 / math.sqrt(INNER * HIDDEN_SIZE)
    return norm_scale / (held[n, HIDDEN_SIZE:, :].astype(jnp.float32) + DAMPING)


def rotate_acts(acts, basis):
    train_v = jnp.dot(acts, basis, preferred_element_type=jnp.float32)
    return train_v.astype(jnp.bfloat16).astype(jnp.float32)


def precondition(qu_ref, ids_ref, query_v, weight, q):
    chosen_v = jnp.where(ids_ref[:, :1] == q, query_v, 0.0).astype(jnp.bfloat16)
    rotated = jnp.dot(qu_ref[...], chosen_v, preferred_element_type=jnp.float32)
    return (rotated * weight).astype(jnp.bfloat16)


def add_score(total, q, u, precond, train_v):
    lanes = lax.broadcasted_iota(jnp.int32, total.shape, 1)
    project = jnp.dot(u, precond, preferred_element_type=jnp.float32)
    score = jnp.sum(project * train_v, axis=1, keepdims=True)
    return total + jnp.where(lanes == q, score, 0.0)


def add_blocks(home, plan, held, acts, u_ref, qu_ref, ids_ref, q_acts, total, kept=None):
    for n, options in enumerate(plan):
        each_option(home, options, lambda copy: copy.wait())
        basis = held[n, :HIDDEN_SIZE, :]
        weight = block_weight(held, n)
        query_v = jnp.dot(q_acts[...], basis, preferred_element_type=jnp.float32)
        train_v = rotate_acts(acts[...], basis)
        for q in range(QUERIES):
            precond = precondition(qu_ref, ids_ref, query_v, weight, q)
            if kept is not None:
                kept[n, pl.ds(q * INNER, INNER), :] = precond
            total = add_score(total, q, u_ref[...], precond, train_v)
    return total


def unpack_rows(rows, b_out, acts, u_ref):
    acts[...] = rows[:, :, :HIDDEN_SIZE].reshape(256, HIDDEN_SIZE)
    u_ref[...] = jnp.dot(
        rows[:, :, HIDDEN_SIZE:].reshape(256, INNER),
        b_out[...],
        preferred_element_type=jnp.float32,
    ).astype(jnp.bfloat16)


def early_kernel(choice, home_ref, rows, b_out, qu_ref, ids_ref, q_acts, *refs):
    count = sum(choice)
    mine_ref, acts, u_ref, kept, held, sems = refs[count:]
    home = home_ref[0] == 1
    plan = fetch_blocks(home, choice, refs[:count], held, sems)
    unpack_rows(rows, b_out, acts, u_ref)
    total = jnp.zeros((256, QUERIES), jnp.float32)
    mine_ref[...] = add_blocks(
        home, plan, held, acts, u_ref, qu_ref, ids_ref, q_acts, total, kept
    )


def late_kernel(acts_a, u_a, acts, u_ref, kept, *refs):
    n_blocks = kept.shape[0]
    sent_ref, acts_all, u_all, held, sems = refs[n_blocks:]
    copies = [
        pltpu.make_async_copy(ref.at[pl.ds(0, HIDDEN_SIZE)], held.at[n], sems.at[n])
        for n, ref in enumerate(refs[:n_blocks])
    ]
    for each in copies:
        each.start()
    acts_all[:256], acts_all[256:] = acts_a[...], acts[...]
    u_all[:256], u_all[256:] = u_a[...], u_ref[...]
    total = jnp.zeros((256, QUERIES), jnp.float32)
    for n, each in enumerate(copies):
        each.wait()
        train_v = rotate_acts(acts[...], held[n])
        for q in range(QUERIES):
            total = add_score(
                total, q, u_ref[...], kept[n, pl.ds(q * INNER, INNER), :], train_v
            )
    sent_ref[...] = total


def score_kernel(
    choice, home_ref, acts, u_ref, qu_ref, ids_ref, q_acts, mine_in, sent_in, *refs
):
    count = sum(choice)
    mine_ref, sent_ref, held, sems = refs[count:]
    home = home_ref[0] == 1
    plan = fetch_blocks(home, choice, refs[:count], held, sems)
    total = jnp.concatenate([mine_in[...], sent_in[...]], axis=0)
    total = add_blocks(home, plan, held, acts, u_ref, qu_ref, ids_ref, q_acts, total)
    mine_ref[...] = total[:256]
    sent_ref[...] = total[256:]


HALF = jax.ShapeDtypeStruct((256, QUERIES), jnp.float32)


def score_cost(n):
    return pl.CostEstimate(flops=n, bytes_accessed=n, transcendentals=0)


ACTS = jax.ShapeDtypeStruct((256, HIDDEN_SIZE), jnp.bfloat16)
GRADS = jax.ShapeDtypeStruct((256, INNER), jnp.bfloat16)


def score_early(home, rows, b_out, queries, blocks):
    choice = tuple(len(options) for options in blocks)
    flat = [x for options in blocks for (x,) in options]
    n = len(blocks)
    return pl.pallas_call(
        functools.partial(early_kernel, choice),
        out_shape=[
            HALF,
            ACTS,
            GRADS,
            jax.ShapeDtypeStruct((n, QUERIES * INNER, 256), jnp.bfloat16),
        ],
        in_specs=[SMEM] + [VMEM] * 5 + [ANY] * len(flat),
        out_specs=[VMEM] * 4,
        scratch_shapes=[
            pltpu.VMEM((n, HIDDEN_SIZE + INNER, 256), jnp.bfloat16),
            pltpu.SemaphoreType.DMA((n,)),
        ],
        compiler_params=pltpu.CompilerParams(vmem_limit_bytes=28 << 20),
        cost_estimate=score_cost(n),
    )(home, rows, b_out, *queries, *flat)


def score_late(acts_a, u_a, acts_b, u_b, kept, blocks):
    n = len(blocks)
    return pl.pallas_call(
        late_kernel,
        out_shape=[
            HALF,
            jax.ShapeDtypeStruct((512, HIDDEN_SIZE), jnp.bfloat16),
            jax.ShapeDtypeStruct((512, INNER), jnp.bfloat16),
        ],
        in_specs=[VMEM] * 5 + [ANY] * n,
        out_specs=[VMEM] * 3,
        scratch_shapes=[
            pltpu.VMEM((n, HIDDEN_SIZE, 256), jnp.bfloat16),
            pltpu.SemaphoreType.DMA((n,)),
        ],
        compiler_params=pltpu.CompilerParams(vmem_limit_bytes=24 << 20),
        cost_estimate=score_cost(n),
    )(acts_a, u_a, acts_b, u_b, kept, *blocks)


def score(home, rows, queries, mine_sum, sent, blocks):
    choice = tuple(len(options) for options in blocks)
    flat = [x for options in blocks for (x,) in options]
    n = len(blocks)
    return pl.pallas_call(
        functools.partial(score_kernel, choice),
        out_shape=[HALF, HALF],
        in_specs=[SMEM] + [VMEM] * 7 + [ANY] * len(flat),
        out_specs=[VMEM] * 2,
        scratch_shapes=[
            pltpu.VMEM((n, HIDDEN_SIZE + INNER, 256), jnp.bfloat16),
            pltpu.SemaphoreType.DMA((n,)),
        ],
        compiler_params=pltpu.CompilerParams(vmem_limit_bytes=24 << 20),
        cost_estimate=score_cost(n),
    )(home, *rows, *queries, mine_sum, sent, *flat)


def on_device(
    train_acts,
    train_grads,
    slot_counts,
    query_acts,
    query_grads,
    query_ids,
    basis_in,
    eigen_vals,
    basis_out,
):
    core, xl, y = lax.axis_index("core"), lax.axis_index("xl"), lax.axis_index("y")
    turn = y // 2
    is_home = core == xl
    home = is_home.astype(jnp.int32).reshape(1)
    groups = route_groups()

    turn_ref = turn.astype(jnp.int32).reshape(1)
    far = pack_block(1 - turn_ref, basis_in, eigen_vals, turn_ref)
    first = send(far, outer_step, cross_step)
    token = other_core(far[:8])
    own = pack_block(turn_ref, basis_in, eigen_vals, token)
    second = send(own, inner_step, cross_step)
    rows = pack_rows(train_acts, train_grads, far)
    rows, own = lax.optimization_barrier((rows, own))
    mine = lax.all_to_all(rows, AXES, 0, 0, axis_index_groups=groups, tiled=True)
    third = send(first, inner_step, outer_step)
    fifth = send(third, None, inner_step)
    q_own, b_own = pack_query(turn_ref, query_ids, query_acts, query_grads, basis_out, first)
    q_acts, b_out, qu, ids = query(home, q_own, other_core(q_own), b_own, other_core(b_own))
    held_second, qu = lax.optimization_barrier((second, qu))
    fourth = send(held_second, None, inner_step)
    queries = (qu, ids, q_acts)
    mine_sum, acts_a, u_a, kept = score_early(
        home, mine, b_out, queries, [[(second,)], [(third,)]]
    )
    acts_a, u_a, fourth = lax.optimization_barrier((acts_a, u_a, fourth))
    acts_b, u_b = other_core(acts_a), other_core(u_a)
    sent, acts, u = score_late(acts_a, u_a, acts_b, u_b, kept, [second, third])
    rows = (acts, u)
    for blocks in ([[(own,), (fourth,)]], [[(first,), (fifth,)]]):
        mine_sum, sent = score(home, rows, queries, mine_sum, sent, blocks)
    mine_sum = mine_sum + other_core(sent)
    back = lax.all_to_all(
        mine_sum.reshape(64, SLOTS, QUERIES), AXES, 0, 0, axis_index_groups=groups, tiled=True
    )
    counts = slot_counts[0].reshape(64)
    live = jnp.arange(SLOTS)[None, :] < counts[:, None]
    return jnp.where(live[:, :, None], back, 0.0).reshape(256, QUERIES).T


def solution(mesh):
    grid = Mesh(mesh.devices.reshape(SIZES), AXES)
    expert, shard = ("xh", "z", "core"), ("xl", "y")
    whole = expert + shard
    in_specs = (
        P(whole, None),
        P(whole, None),
        P(whole, None, None),
        P(None, expert, None, None),
        P(None, expert, None, None),
        P(None, expert, None),
        P(None, expert, None, shard),
        P(None, expert, None, shard),
        P(None, expert, None, None),
    )
    return jax.shard_map(
        on_device, mesh=grid, in_specs=in_specs, out_specs=P(None, whole), check_vma=False
    )
```
